1024 devices in a mesh: dp: 16 (over y, z_hi), tensor: 64 (over x, z_lo, core).
Axes of the slice: x: 4, y: 8, z: 16 (z_hi: 2, z_lo: 8; z = z_hi * 8 + z_lo), core: 2. Of those that a mesh axis runs over, the one named last changes fastest.
Arguments:
- gate_input: bfloat16 [2048, 16384], P('dp', 'tensor'), may hold values from -6 to 6
- up_input: bfloat16 [2048, 16384], P('dp', 'tensor'), may hold values from -6 to 6
- residual: bfloat16 [2048, 4096], P('dp', 'tensor'), may hold values from -6 to 6
- down_proj: bfloat16 [16384, 4096], P('tensor', 'dp'), may hold values from -0.125 to 0.125
- cotangent: bfloat16 [2048, 4096], P('dp', 'tensor'), may hold values from -16 to 16
Outputs:
- layer_out: bfloat16 [2048, 4096], P('dp', 'tensor')
- gate_grad: bfloat16 [2048, 16384], P('dp', 'tensor')
- up_grad: bfloat16 [2048, 16384], P('dp', 'tensor')
- down_grad: bfloat16 [16384, 4096], P('tensor', 'dp')
The draws below stay inside these ranges and needn't reach their ends.
All inputs are finite; a program needn't handle non-finite values.
Results may differ from the reference program's by a relative error of at most 0.02.
Values may be sent and summed in bfloat16 or wider, within the bound.
No kernel may reach another device: no remote copies, remote signals or barrier semaphores. Data moves between devices by JAX's collectives and lax.ppermute only.
A program may use at most 32 MiB of HBM per device.

```python
import math
import jax
import jax.numpy as jnp
from jax import lax

DW = 4096
FF = 16384
TOK_DEV = 128
TOKENS = 2048
N_DP = 16


def with_spikes(result, stream_key, source, target, shards_of, factor):
    owner, partner = [(jnp.arange(result.shape[position]) // (result.shape[position] // shards_of)).reshape([-1 if axis == position else 1 for axis in range(result.ndim)]) for position in (source, target)]
    chosen = jax.random.permutation(stream_key, shards_of)[partner]
    strong = (owner == chosen) | (owner == (partner + shards_of // 2) % shards_of)
    return jnp.where(strong, factor * result, result)


def block_levels(rng, shape, split, low, top_value):
    def one(axis_at, blocks):
        draws = jax.random.uniform(jax.random.fold_in(jax.random.fold_in(rng, 6), axis_at), (blocks,), jnp.float32, low / len(split), top_value / len(split))
        return jnp.repeat(jnp.exp(draws), shape[axis_at] // blocks).reshape((-1,) + (1,) * (len(shape) - axis_at - 1))

    gain = one(*split[0])
    for cut in split[1:]:
        gain = gain * one(*cut)
    return gain


def centred(rng, dims, scale, reach, split=(), kind=jnp.bfloat16):
    array = jax.random.normal(rng, dims, jnp.float32) * scale
    if len(split) > 0:
        array = block_levels(rng, dims, split, -0.22, 0.18) * array
    return jnp.clip(array, min=-reach, max=reach).astype(kind)


def gaussian_with(own_key, extent, deviation, reach, split, heavy, dtype=jnp.bfloat16):
    result = deviation * jax.random.normal(own_key, extent, jnp.float32)
    if split:
        result = result * block_levels(own_key, extent, split, -0.22, 0.18)
    return jnp.clip(with_spikes(result, jax.random.fold_in(own_key, 3), *heavy), -reach, reach).astype(dtype)


def setup_inputs(seed: int = 0) -> dict:
    splits = jax.random.split(jax.random.key(seed), 6)
    gate_input = centred(splits[0], (TOKENS, FF), 1.0, 6.0, ((0, 16), (1, 64)))
    up_input = centred(splits[1], (TOKENS, FF), 1.0, 6.0, ((0, 16), (1, 64)))
    residual = centred(splits[2], (TOKENS, DW), 1.0, 6.0, ((0, 16), (1, 64)))
    down_proj = gaussian_with(splits[3], (FF, DW), FF ** -0.5, 0.125, ((0, 64), (1, 16)), (0, 1, 64, 4.0))
    cotangent = gaussian_with(splits[4], (TOKENS, DW), 1.0, 16.0, ((0, 16), (1, 64)), (0, 1, 64, 4.0))
    return dict(gate_input=gate_input, up_input=up_input, residual=residual, down_proj=down_proj, cotangent=cotangent)


def reference(gate_input, up_input, residual, down_proj, cotangent):
    gate_values = gate_input.astype(jnp.float32)
    up_values = up_input.astype(jnp.float32)
    sigmoid_gate = jax.nn.sigmoid(gate_values)
    hidden = (gate_values * sigmoid_gate * up_values).astype(jnp.bfloat16)
    projected = jnp.dot(hidden, down_proj, preferred_element_type=jnp.float32)
    layer_out = (residual.astype(jnp.float32) + projected).astype(jnp.bfloat16)
    hidden_grad = lax.dot_general(cotangent, down_proj, (((1,), (1,)), ((), ())), preferred_element_type=jnp.float32)
    up_grad = (hidden_grad * gate_values * sigmoid_gate).astype(jnp.bfloat16)
    gate_grad = (hidden_grad * up_values * sigmoid_gate * (1.0 + gate_values * (1.0 - sigmoid_gate))).astype(jnp.bfloat16)
    hidden_groups = hidden.reshape(N_DP, TOK_DEV, FF)
    cot_groups = cotangent.reshape(N_DP, TOK_DEV, DW)

    def add_group(running, operands):
        hidden_piece, cot_piece = operands
        group_term = lax.dot_general(hidden_piece, cot_piece, (((0,), (0,)), ((), ())), preferred_element_type=jnp.float32)
        group_term = lax.optimization_barrier(group_term.astype(jnp.bfloat16))
        return (running + group_term.astype(jnp.float32), None)
    running = lax.scan(add_group, jnp.zeros((FF, DW), jnp.float32), (hidden_groups, cot_groups))[0]
    down_grad = (running * (1.0 / math.sqrt(TOKENS))).astype(jnp.bfloat16)
    return (layer_out, gate_grad, up_grad, down_grad)
```

```python
import math

import jax
import jax.numpy as jnp
from jax import lax
from jax.sharding import Mesh
from jax.sharding import PartitionSpec as P

AXES = ("y", "zh", "x", "zl", "c")
SIZES = (8, 2, 4, 8, 2)
BF, F32 = jnp.bfloat16, jnp.float32


def swap_pairs():
    def at(y, zh, x, zl, c):
        return (((y * 2 + zh) * 4 + x) * 8 + zl) * 2 + c

    return [
        (at(y, zh, x, zl, c), at(2 * x + zl // 4, zh, y // 2, 4 * (y % 2) + zl % 4, c))
        for y in range(8)
        for zh in range(2)
        for x in range(4)
        for zl in range(8)
        for c in range(2)
    ]


def gather(part, axis):
    return lax.all_to_all(jnp.broadcast_to(part[None], (lax.axis_size(axis),) + part.shape), axis, 0, 0)


def scatter_sum(parts, axis):
    return jnp.sum(lax.all_to_all(parts, axis, 0, 0).astype(F32), axis=0)


def body(gate_input, up_input, residual, down_proj, cotangent):
    swap = swap_pairs()
    zh = lax.axis_index("zh")
    across = [(0, 1), (1, 0)]
    weights_other = lax.ppermute(down_proj, "zh", across)
    cot_moved = lax.ppermute(cotangent.T, AXES, swap)

    gate = gate_input.astype(F32)
    up = up_input.astype(F32)
    sig = jax.nn.sigmoid(gate)
    hidden = (gate * sig * up).astype(BF)

    hid = gather(hidden, "y")
    cot = gather(gather(gather(cot_moved, "zl"), "x"), "c")
    cot = cot.reshape(2, 4, 2, 4, 64, 128)

    low = jnp.where(zh == 0, down_proj, weights_other)
    high = jnp.where(zh == 0, weights_other, down_proj)
    weights = jnp.concatenate([low, high], axis=1).reshape(256, 4, 2, 64)

    proj = jnp.einsum(
        "klcf,xhtk->cxhlft", weights, hid.reshape(4, 2, 128, 256), preferred_element_type=F32
    ).astype(BF)
    proj = scatter_sum(proj, "c").astype(BF)
    proj = scatter_sum(proj, "x").astype(BF)
    proj = scatter_sum(proj.reshape(8, 64, 128), "zl")
    proj = lax.ppermute(proj, AXES, swap)
    layer_out = (residual.astype(F32).T + proj).astype(BF).T

    cot_rows = jnp.transpose(cot, (3, 0, 4, 1, 2, 5)).reshape(512, 1024)
    partial = lax.dot_general(
        cot_rows, weights.reshape(256, 512), (((0,), (1,)), ((), ())), preferred_element_type=F32
    ).astype(BF)
    hidden_grad = scatter_sum(partial.reshape(8, 128, 256), "y")
    up_grad = (hidden_grad * gate * sig).astype(BF)
    gate_grad = (hidden_grad * up * sig * (1.0 + gate * (1.0 - sig))).astype(BF)

    hid_rows = hid.reshape(1024, 256)

    def term(which):
        feats = lax.dynamic_slice_in_dim(cot_rows, which * 256, 256, 0)
        return lax.dot_general(hid_rows, feats, (((0,), (1,)), ((), ())), preferred_element_type=F32)

    arrived = lax.ppermute(term(1 - zh).astype(BF), "zh", across)
    down_grad = ((term(zh) + arrived.astype(F32)) * (1.0 / math.sqrt(2048))).astype(BF)
    return (layer_out, gate_grad, up_grad, down_grad)


def solution(mesh):
    fine = Mesh(mesh.devices.reshape(SIZES), AXES)
    dp, tensor = ("y", "zh"), ("x", "zl", "c")
    in_specs = (P(dp, tensor), P(dp, tensor), P(dp, tensor), P(tensor, dp), P(dp, tensor))
    out_specs = (P(dp, tensor), P(dp, tensor), P(dp, tensor), P(tensor, dp))
    return jax.shard_map(body, mesh=fine, in_specs=in_specs, out_specs=out_specs, check_vma=False)
```

```python
import math

import jax
import jax.numpy as jnp
from jax import lax
from jax.experimental import pallas as pl
from jax.experimental.pallas import tpu as pltpu
from jax.sharding import Mesh
from jax.sharding import PartitionSpec as P

AXES = ("y", "zh", "x", "zl", "c")
SIZES = (8, 2, 4, 8, 2)
BF, F32 = jnp.bfloat16, jnp.float32
ACROSS = [(0, 1), (1, 0)]


def swap_pairs():
    def at(y, zh, x, zl, c):
        return (((y * 2 + zh) * 4 + x) * 8 + zl) * 2 + c

    return [
        (at(y, zh, x, zl, c), at(2 * x + zl // 4, zh, y // 2, 4 * (y % 2) + zl % 4, c))
        for y in range(8)
        for zh in range(2)
        for x in range(4)
        for zl in range(8)
        for c in range(2)
    ]


def in_vmem(kernel, out_shapes, flops, *operands, scratch=()):
    spec = pl.BlockSpec(memory_space=pltpu.VMEM)
    moved = sum(math.prod(a.shape) * a.dtype.itemsize for a in (*operands, *out_shapes))
    return pl.pallas_call(
        kernel,
        out_shape=out_shapes,
        in_specs=[spec] * len(operands),
        out_specs=[spec] * len(out_shapes),
        scratch_shapes=list(scratch),
        compiler_params=pltpu.CompilerParams(vmem_limit_bytes=32 * 1024 * 1024),
        cost_estimate=pl.CostEstimate(flops=flops, bytes_accessed=moved, transcendentals=0),
    )(*operands)


def shape(dims, dtype=BF):
    return jax.ShapeDtypeStruct(dims, dtype)


def hidden_kernel(gate_ref, up_ref, out_ref):
    gate = gate_ref[...].astype(F32)
    hidden = (gate * jax.nn.sigmoid(gate) * up_ref[...].astype(F32)).astype(BF)
    for i in range(8):
        out_ref[i] = hidden


def proj_kernel(hid_ref, own_ref, other_ref, keep_ref, send_ref):
    zh, core = lax.axis_index("zh"), lax.axis_index("c")
    hid = hid_ref[...].reshape(1024, 256)
    for l in range(4):
        cols = slice((l % 2) * 128, (l % 2) * 128 + 128)
        w = jnp.where(zh == l // 2, own_ref[:, cols], other_ref[:, cols])
        res = lax.dot_general(w, hid, (((0,), (1,)), ((), ())), preferred_element_type=F32).astype(BF)
        first, second = res[:64], res[64:]
        keep = jnp.where(core == 0, first, second)
        send = jnp.where(core == 0, second, first)
        for g in range(8):
            toks = slice(g * 128, g * 128 + 128)
            keep_ref[g // 2, (g % 2) * 4 + l] = keep[:, toks]
            send_ref[g // 2, (g % 2) * 4 + l] = send[:, toks]


def grad_kernel(hid_ref, cot_ref, own_ref, other_ref, partial_ref, keep_ref, send_ref, rows_ref):
    zh = lax.axis_index("zh")
    for g in range(8):
        for l in range(4):
            for c in range(2):
                rows_ref[(2 * l + c) * 64 : (2 * l + c) * 64 + 64, g * 128 : g * 128 + 128] = cot_ref[
                    g // 2, c, (g % 2) * 4 + l
                ]
    own, other = own_ref[...], other_ref[...]
    low = jnp.where(zh == 0, own, other)
    high = jnp.where(zh == 0, other, own)
    weights = jnp.concatenate([low, high], axis=1)
    for g in range(8):
        partial_ref[g] = lax.dot_general(
            rows_ref[:, g * 128 : g * 128 + 128],
            weights,
            (((0,), (1,)), ((), ())),
            preferred_element_type=F32,
        ).astype(BF)
    hid = hid_ref[...].reshape(1024, 256)
    first = lax.dot_general(hid, rows_ref[:256], (((0,), (1,)), ((), ())), preferred_element_type=F32)
    second = lax.dot_general(hid, rows_ref[256:], (((0,), (1,)), ((), ())), preferred_element_type=F32)
    keep_ref[...] = jnp.where(zh == 0, first, second)
    send_ref[...] = jnp.where(zh == 0, second, first).astype(BF)


def after(value, *deps):
    return lax.optimization_barrier((value, *deps))[0]


def gather(part, axis):
    return lax.all_to_all(jnp.broadcast_to(part[None], (lax.axis_size(axis),) + part.shape), axis, 0, 0)


def scatter_sum(parts, axis):
    return jnp.sum(lax.all_to_all(parts, axis, 0, 0).astype(F32), axis=0)


def body(gate_input, up_input, residual, down_proj, cotangent):
    swap = swap_pairs()
    cot_moved = lax.ppermute(cotangent.T, AXES, swap)
    w_other = lax.ppermute(down_proj, "zh", ACROSS)

    (spread,) = in_vmem(hidden_kernel, [shape((8, 128, 256))], 500_000, gate_input, up_input)
    hid = lax.all_to_all(spread, "y", 0, 0)

    cot_line = gather(after(cot_moved, hid), "zl")
    cot = lax.all_gather(cot_line, ("x", "c"), axis=0, tiled=False)
    cot = cot.reshape(4, 2, 8, 64, 128)

    hid_now, w_now = lax.optimization_barrier((hid, w_other, cot_line))[:2]
    keep, send = in_vmem(
        proj_kernel, [shape((4, 8, 64, 128))] * 2, 2 * 1024 * 256 * 512, hid_now, down_proj, w_now
    )
    proj = (keep.astype(F32) + lax.ppermute(send, "c", ACROSS).astype(F32)).astype(BF)
    proj = scatter_sum(proj, "x").astype(BF)
    proj = scatter_sum(proj, "zl")

    cot_now = after(cot, proj)
    partial, term, term_out = in_vmem(
        grad_kernel,
        [shape((8, 128, 256)), shape((256, 256), F32), shape((256, 256))],
        4 * 1024 * 256 * 512,
        hid,
        cot_now,
        down_proj,
        w_now,
        scratch=[pltpu.VMEM((512, 1024), BF)],
    )
    moved = lax.ppermute(proj, AXES, swap)
    term_in = lax.ppermute(term_out, "zh", ACROSS)
    hidden_grad = scatter_sum(partial, "y")

    gate = gate_input.astype(F32)
    up = up_input.astype(F32)
    sig = jax.nn.sigmoid(gate)
    up_grad = (hidden_grad * gate * sig).astype(BF)
    gate_grad = (hidden_grad * up * sig * (1.0 + gate * (1.0 - sig))).astype(BF)
    layer_out = (residual.astype(F32).T + moved).astype(BF).T
    down_grad = ((term + term_in.astype(F32)) * (1.0 / math.sqrt(2048))).astype(BF)
    return (layer_out, gate_grad, up_grad, down_grad)


def solution(mesh):
    fine = Mesh(mesh.devices.reshape(SIZES), AXES)
    dp, tensor = ("y", "zh"), ("x", "zl", "c")
    in_specs = (P(dp, tensor), P(dp, tensor), P(dp, tensor), P(tensor, dp), P(dp, tensor))
    out_specs = (P(dp, tensor), P(dp, tensor), P(dp, tensor), P(tensor, dp))
    return jax.shard_map(body, mesh=fine, in_specs=in_specs, out_specs=out_specs, check_vma=False)
```

```python
import math

import jax
import jax.numpy as jnp
from jax import lax
from jax.experimental import pallas as pl
from jax.experimental.pallas import tpu as pltpu
from jax.sharding import Mesh
from jax.sharding import PartitionSpec as P

AXES = ("y", "zh", "x", "zl", "c")
SIZES = (8, 2, 4, 8, 2)
BF, F32 = jnp.bfloat16, jnp.float32
ACROSS = [(0, 1), (1, 0)]


def swap_pairs():
    def at(y, zh, x, zl, c):
        return (((y * 2 + zh) * 4 + x) * 8 + zl) * 2 + c

    return [
        (at(y, zh, x, zl, c), at(2 * x + zl // 4, zh, y // 2, 4 * (y % 2) + zl % 4, c))
        for y in range(8)
        for zh in range(2)
        for x in range(4)
        for zl in range(8)
        for c in range(2)
    ]


def in_vmem(kernel, out_shapes, flops, *operands, scratch=()):
    spec = pl.BlockSpec(memory_space=pltpu.VMEM)
    moved = sum(math.prod(a.shape) * a.dtype.itemsize for a in (*operands, *out_shapes))
    return pl.pallas_call(
        kernel,
        out_shape=out_shapes,
        in_specs=[spec] * len(operands),
        out_specs=[spec] * len(out_shapes),
        scratch_shapes=list(scratch),
        compiler_params=pltpu.CompilerParams(vmem_limit_bytes=32 * 1024 * 1024),
        cost_estimate=pl.CostEstimate(flops=flops, bytes_accessed=moved, transcendentals=0),
    )(*operands)


def shape(dims, dtype=BF):
    return jax.ShapeDtypeStruct(dims, dtype)


def hidden_kernel(gate_ref, up_ref, out_ref):
    gate = gate_ref[...].astype(F32)
    hidden = (gate * jax.nn.sigmoid(gate) * up_ref[...].astype(F32)).astype(BF)
    for i in range(8):
        out_ref[i] = hidden


def proj_kernel(hid_ref, own_ref, other_ref, keep_ref, send_ref):
    zh, core = lax.axis_index("zh"), lax.axis_index("c")
    hid = hid_ref[...].reshape(1024, 256)
    for l in range(4):
        cols = slice((l % 2) * 128, (l % 2) * 128 + 128)
        w = jnp.where(zh == l // 2, own_ref[:, cols], other_ref[:, cols])
        res = lax.dot_general(w, hid, (((0,), (1,)), ((), ())), preferred_element_type=F32).astype(BF)
        first, second = res[:64], res[64:]
        keep = jnp.where(core == 0, first, second)
        send = jnp.where(core == 0, second, first)
        for g in range(8):
            toks = slice(g * 128, g * 128 + 128)
            keep_ref[g // 2, (g % 2) * 4 + l] = keep[:, toks]
            send_ref[g // 2, (g % 2) * 4 + l] = send[:, toks]


def pack_kernel(cot_ref, keep_ref, came_ref, out_ref):
    total = (keep_ref[...].astype(F32) + came_ref[...].astype(F32)).astype(BF)
    for x in range(4):
        out_ref[x, :8] = cot_ref[...]
        out_ref[x, 8:] = total[x]


def unpack_kernel(got_ref, cot_ref, sum_ref):
    cot_ref[...] = got_ref[:, :8]
    sum_ref[...] = jnp.sum(got_ref[:, 8:].astype(F32), axis=0).astype(BF)


def grad_kernel(hid_ref, mine_ref, its_ref, own_ref, other_ref, partial_ref, keep_ref, send_ref, rows_ref):
    zh, core = lax.axis_index("zh"), lax.axis_index("c")
    for l in range(4):
        here = pl.ds(pl.multiple_of((2 * l + core) * 64, 64), 64)
        there = pl.ds(pl.multiple_of((2 * l + 1 - core) * 64, 64), 64)
        for g in range(8):
            toks = slice(g * 128, g * 128 + 128)
            rows_ref[here, toks] = mine_ref[g // 2, (g % 2) * 4 + l]
            rows_ref[there, toks] = its_ref[g // 2, (g % 2) * 4 + l]
    own, other = own_ref[...], other_ref[...]
    low = jnp.where(zh == 0, own, other)
    high = jnp.where(zh == 0, other, own)
    weights = jnp.concatenate([low, high], axis=1)
    for g in range(8):
        partial_ref[g] = lax.dot_general(
            rows_ref[:, g * 128 : g * 128 + 128],
            weights,
            (((0,), (1,)), ((), ())),
            preferred_element_type=F32,
        ).astype(BF)
    hid = hid_ref[...].reshape(1024, 256)
    first = lax.dot_general(hid, rows_ref[:256], (((0,), (1,)), ((), ())), preferred_element_type=F32)
    second = lax.dot_general(hid, rows_ref[256:], (((0,), (1,)), ((), ())), preferred_element_type=F32)
    keep_ref[...] = jnp.where(zh == 0, first, second)
    send_ref[...] = jnp.where(zh == 0, second, first).astype(BF)


def after(value, *deps):
    return lax.optimization_barrier((value, *deps))[0]


def gather(part, axis):
    return lax.all_to_all(jnp.broadcast_to(part[None], (lax.axis_size(axis),) + part.shape), axis, 0, 0)


def scatter_sum(parts, axis):
    return jnp.sum(lax.all_to_all(parts, axis, 0, 0).astype(F32), axis=0)


def body(gate_input, up_input, residual, down_proj, cotangent):
    swap = swap_pairs()
    cot_moved = lax.ppermute(cotangent.T, AXES, swap)
    w_other = lax.ppermute(down_proj, "zh", ACROSS)

    (spread,) = in_vmem(hidden_kernel, [shape((8, 128, 256))], 500_000, gate_input, up_input)
    hid = lax.all_to_all(spread, "y", 0, 0)

    cot_moved, w_now = lax.optimization_barrier((cot_moved, w_other, hid))[:2]
    cot_line = gather(cot_moved, "zl")

    keep, send = in_vmem(
        proj_kernel,
        [shape((4, 8, 64, 128))] * 2,
        2 * 1024 * 256 * 512,
        after(hid, cot_line),
        down_proj,
        w_now,
    )
    came = lax.ppermute(send, "c", ACROSS)
    (packed,) = in_vmem(pack_kernel, [shape((4, 16, 64, 128))], 300_000, cot_line, keep, came)
    mine, proj = in_vmem(
        unpack_kernel,
        [shape((4, 8, 64, 128)), shape((8, 64, 128))],
        300_000,
        lax.all_to_all(packed, "x", 0, 0),
    )
    its = lax.ppermute(mine, "c", ACROSS)
    proj = scatter_sum(proj, "zl")
    partial, term, term_out = in_vmem(
        grad_kernel,
        [shape((8, 128, 256)), shape((256, 256), F32), shape((256, 256))],
        4 * 1024 * 256 * 512,
        hid,
        mine,
        after(its, proj),
        down_proj,
        w_now,
        scratch=[pltpu.VMEM((512, 1024), BF)],
    )
    moved = lax.ppermute(proj, AXES, swap)
    term_in = lax.ppermute(term_out, "zh", ACROSS)
    hidden_grad = scatter_sum(partial, "y")

    gate = gate_input.astype(F32)
    up = up_input.astype(F32)
    sig = jax.nn.sigmoid(gate)
    up_grad = (hidden_grad * gate * sig).astype(BF)
    gate_grad = (hidden_grad * up * sig * (1.0 + gate * (1.0 - sig))).astype(BF)
    layer_out = (residual.astype(F32).T + moved).astype(BF).T
    down_grad = ((term + term_in.astype(F32)) * (1.0 / math.sqrt(2048))).astype(BF)
    return (layer_out, gate_grad, up_grad, down_grad)


def solution(mesh):
    fine = Mesh(mesh.devices.reshape(SIZES), AXES)
    dp, tensor = ("y", "zh"), ("x", "zl", "c")
    in_specs = (P(dp, tensor), P(dp, tensor), P(dp, tensor), P(tensor, dp), P(dp, tensor))
    out_specs = (P(dp, tensor), P(dp, tensor), P(dp, tensor), P(tensor, dp))
    return jax.shard_map(body, mesh=fine, in_specs=in_specs, out_specs=out_specs, check_vma=False)
```

```python
import math

import jax
import jax.numpy as jnp
from jax import lax
from jax.experimental import pallas as pl
from jax.experimental.pallas import tpu as pltpu
from jax.sharding import Mesh
from jax.sharding import PartitionSpec as P

AXES = ("y", "zh", "x", "zl", "c")
SIZES = (8, 2, 4, 8, 2)
BF, F32 = jnp.bfloat16, jnp.float32
ACROSS = [(0, 1), (1, 0)]


def swap_pairs():
    def at(y, zh, x, zl, c):
        return (((y * 2 + zh) * 4 + x) * 8 + zl) * 2 + c

    return [
        (at(y, zh, x, zl, c), at(2 * x + zl // 4, zh, y // 2, 4 * (y % 2) + zl % 4, c))
        for y in range(8)
        for zh in range(2)
        for x in range(4)
        for zl in range(8)
        for c in range(2)
    ]


def in_vmem(kernel, out_shapes, flops, *operands, scratch=()):
    spec = pl.BlockSpec(memory_space=pltpu.VMEM)
    moved = sum(math.prod(a.shape) * a.dtype.itemsize for a in (*operands, *out_shapes))
    return pl.pallas_call(
        kernel,
        out_shape=out_shapes,
        in_specs=[spec] * len(operands),
        out_specs=[spec] * len(out_shapes),
        scratch_shapes=list(scratch),
        compiler_params=pltpu.CompilerParams(vmem_limit_bytes=32 * 1024 * 1024),
        cost_estimate=pl.CostEstimate(flops=flops, bytes_accessed=moved, transcendentals=0),
    )(*operands)


def shape(dims, dtype=BF):
    return jax.ShapeDtypeStruct(dims, dtype)


def hidden_kernel(gate_ref, up_ref, out_ref):
    gate = gate_ref[...].astype(F32)
    hidden = (gate * jax.nn.sigmoid(gate) * up_ref[...].astype(F32)).astype(BF)
    for i in range(8):
        out_ref[i] = hidden


def proj_kernel(hid_ref, own_ref, other_ref, keep_ref, send_ref):
    zh, core = lax.axis_index("zh"), lax.axis_index("c")
    hid = hid_ref[...].reshape(1024, 256)
    for l in range(4):
        cols = slice((l % 2) * 128, (l % 2) * 128 + 128)
        w = jnp.where(zh == l // 2, own_ref[:, cols], other_ref[:, cols])
        res = lax.dot_general(w, hid, (((0,), (1,)), ((), ())), preferred_element_type=F32).astype(BF)
        first, second = res[:64], res[64:]
        keep = jnp.where(core == 0, first, second)
        send = jnp.where(core == 0, second, first)
        for g in range(8):
            toks = slice(g * 128, g * 128 + 128)
            keep_ref[g // 2, (g % 2) * 4 + l] = keep[:, toks]
            send_ref[g // 2, (g % 2) * 4 + l] = send[:, toks]


def pack_kernel(cot_ref, keep_ref, came_ref, out_ref):
    total = (keep_ref[...].astype(F32) + came_ref[...].astype(F32)).astype(BF)
    for x in range(4):
        out_ref[x, :8] = cot_ref[...]
        out_ref[x, 8:] = total[x]


def unpack_kernel(got_ref, cot_ref, sum_ref):
    cot_ref[...] = got_ref[:, :8]
    sum_ref[...] = jnp.sum(got_ref[:, 8:].astype(F32), axis=0).astype(BF)


def grad_kernel(hid_ref, mine_ref, its_ref, own_ref, other_ref, partial_ref, keep_ref, send_ref, rows_ref):
    zh, core = lax.axis_index("zh"), lax.axis_index("c")
    for l in range(4):
        here = pl.ds(pl.multiple_of((2 * l + core) * 64, 64), 64)
        there = pl.ds(pl.multiple_of((2 * l + 1 - core) * 64, 64), 64)
        for g in range(8):
            toks = slice(g * 128, g * 128 + 128)
            rows_ref[here, toks] = mine_ref[g // 2, (g % 2) * 4 + l]
            rows_ref[there, toks] = its_ref[g // 2, (g % 2) * 4 + l]
    own, other = own_ref[...], other_ref[...]
    low = jnp.where(zh == 0, own, other)
    high = jnp.where(zh == 0, other, own)
    weights = jnp.concatenate([low, high], axis=1)
    for g in range(8):
        partial_ref[g] = lax.dot_general(
            rows_ref[:, g * 128 : g * 128 + 128],
            weights,
            (((0,), (1,)), ((), ())),
            preferred_element_type=F32,
        ).astype(BF)
    hid = hid_ref[...].reshape(1024, 256)
    first = lax.dot_general(hid, rows_ref[:256], (((0,), (1,)), ((), ())), preferred_element_type=F32)
    second = lax.dot_general(hid, rows_ref[256:], (((0,), (1,)), ((), ())), preferred_element_type=F32)
    keep_ref[...] = jnp.where(zh == 0, first, second)
    send_ref[...] = jnp.where(zh == 0, second, first).astype(BF)


def after(value, *deps):
    return lax.optimization_barrier((value, *deps))[0]


def gather(part, axis):
    return lax.all_to_all(jnp.broadcast_to(part[None], (lax.axis_size(axis),) + part.shape), axis, 0, 0)


def scatter_sum(parts, axis):
    return jnp.sum(lax.all_to_all(parts, axis, 0, 0).astype(F32), axis=0)


def body(gate_input, up_input, residual, down_proj, cotangent):
    swap = swap_pairs()
    cot_moved = lax.ppermute(cotangent.T, AXES, swap)
    w_other = lax.ppermute(down_proj, "zh", ACROSS)

    spread = pl.pallas_call(
        hidden_kernel,
        out_shape=shape((8, 128, 256)),
        cost_estimate=pl.CostEstimate(flops=500_000, bytes_accessed=700_000, transcendentals=0),
    )(gate_input, up_input)
    hid = lax.all_to_all(spread, "y", 0, 0)

    cot_moved, w_now, hid = lax.optimization_barrier((cot_moved, w_other, hid))
    cot_line = gather(cot_moved, "zl")

    keep, send = in_vmem(
        proj_kernel,
        [shape((4, 8, 64, 128))] * 2,
        2 * 1024 * 256 * 512,
        hid,
        down_proj,
        w_now,
    )
    came = lax.ppermute(send, "c", ACROSS)
    (packed,) = in_vmem(pack_kernel, [shape((4, 16, 64, 128))], 300_000, cot_line, keep, came)
    mine, proj = in_vmem(
        unpack_kernel,
        [shape((4, 8, 64, 128)), shape((8, 64, 128))],
        300_000,
        lax.all_to_all(packed, "x", 0, 0),
    )
    its = lax.ppermute(mine, "c", ACROSS)
    proj = scatter_sum(proj, "zl")
    partial, term, term_out = in_vmem(
        grad_kernel,
        [shape((8, 128, 256)), shape((256, 256), F32), shape((256, 256))],
        4 * 1024 * 256 * 512,
        hid,
        mine,
        its,
        down_proj,
        w_now,
        scratch=[pltpu.VMEM((512, 1024), BF)],
    )
    moved = lax.ppermute(proj, AXES, swap)
    term_in = lax.ppermute(after(term_out, proj), "zh", ACROSS)
    hidden_grad = scatter_sum(after(partial, proj), "y")

    gate = gate_input.astype(F32)
    up = up_input.astype(F32)
    sig = jax.nn.sigmoid(gate)
    up_grad = (hidden_grad * gate * sig).astype(BF)
    gate_grad = (hidden_grad * up * sig * (1.0 + gate * (1.0 - sig))).astype(BF)
    layer_out = (residual.astype(F32).T + moved).astype(BF).T
    down_grad = ((term + term_in.astype(F32)) * (1.0 / math.sqrt(2048))).astype(BF)
    return (layer_out, gate_grad, up_grad, down_grad)


def solution(mesh):
    fine = Mesh(mesh.devices.reshape(SIZES), AXES)
    dp, tensor = ("y", "zh"), ("x", "zl", "c")
    in_specs = (P(dp, tensor), P(dp, tensor), P(dp, tensor), P(tensor, dp), P(dp, tensor))
    out_specs = (P(dp, tensor), P(dp, tensor), P(dp, tensor), P(tensor, dp))
    return jax.shard_map(body, mesh=fine, in_specs=in_specs, out_specs=out_specs, check_vma=False)
```

```python
import math

import jax
import jax.numpy as jnp
from jax import lax
from jax.experimental import pallas as pl
from jax.experimental.pallas import tpu as pltpu
from jax.sharding import Mesh
from jax.sharding import PartitionSpec as P

AXES = ("y", "zh", "x", "zl", "c")
SIZES = (8, 2, 4, 8, 2)
BF, F32 = jnp.bfloat16, jnp.float32
ACROSS = [(0, 1), (1, 0)]


def swap_pairs():
    def at(y, zh, x, zl, c):
        return (((y * 2 + zh) * 4 + x) * 8 + zl) * 2 + c

    return [
        (at(y, zh, x, zl, c), at(2 * x + zl // 4, zh, y // 2, 4 * (y % 2) + zl % 4, c))
        for y in range(8)
        for zh in range(2)
        for x in range(4)
        for zl in range(8)
        for c in range(2)
    ]


def in_vmem(kernel, out_shapes, flops, *operands, scratch=()):
    spec = pl.BlockSpec(memory_space=pltpu.VMEM)
    moved = sum(math.prod(a.shape) * a.dtype.itemsize for a in (*operands, *out_shapes))
    return pl.pallas_call(
        kernel,
        out_shape=out_shapes,
        in_specs=[spec] * len(operands),
        out_specs=[spec] * len(out_shapes),
        scratch_shapes=list(scratch),
        compiler_params=pltpu.CompilerParams(vmem_limit_bytes=32 * 1024 * 1024),
        cost_estimate=pl.CostEstimate(flops=flops, bytes_accessed=moved, transcendentals=0),
    )(*operands)


def shape(dims, dtype=BF):
    return jax.ShapeDtypeStruct(dims, dtype)


def hidden_kernel(gate_ref, up_ref, out_ref):
    gate = gate_ref[...].astype(F32)
    hidden = (gate * jax.nn.sigmoid(gate) * up_ref[...].astype(F32)).astype(BF)
    for i in range(8):
        out_ref[i] = hidden


def proj_kernel(hid_ref, own_ref, other_ref, keep_ref, send_ref):
    zh, core = lax.axis_index("zh"), lax.axis_index("c")
    hid = hid_ref[...].reshape(1024, 256)
    for l in range(4):
        cols = slice((l % 2) * 128, (l % 2) * 128 + 128)
        w = jnp.where(zh == l // 2, own_ref[:, cols], other_ref[:, cols])
        res = lax.dot_general(w, hid, (((0,), (1,)), ((), ())), preferred_element_type=F32).astype(BF)
        first, second = res[:64], res[64:]
        keep = jnp.where(core == 0, first, second)
        send = jnp.where(core == 0, second, first)
        for g in range(8):
            toks = slice(g * 128, g * 128 + 128)
            keep_ref[g // 2, (g % 2) * 4 + l] = keep[:, toks]
            send_ref[g // 2, (g % 2) * 4 + l] = send[:, toks]


def pack_kernel(cot_ref, keep_ref, came_ref, out_ref):
    total = (keep_ref[...].astype(F32) + came_ref[...].astype(F32)).astype(BF)
    for x in range(4):
        out_ref[x, :8] = cot_ref[...]
        out_ref[x, 8:] = total[x]


def unpack_kernel(got_ref, cot_ref, sum_ref):
    cot_ref[...] = got_ref[:, :8]
    sum_ref[...] = jnp.sum(got_ref[:, 8:].astype(F32), axis=0).astype(BF)


def grad_kernel(hid_ref, mine_ref, its_ref, own_ref, other_ref, partial_ref, keep_ref, send_ref, rows_ref):
    zh, core = lax.axis_index("zh"), lax.axis_index("c")
    for l in range(4):
        here = pl.ds(pl.multiple_of((2 * l + core) * 64, 64), 64)
        there = pl.ds(pl.multiple_of((2 * l + 1 - core) * 64, 64), 64)
        for g in range(8):
            toks = slice(g * 128, g * 128 + 128)
            rows_ref[here, toks] = mine_ref[g // 2, (g % 2) * 4 + l]
            rows_ref[there, toks] = its_ref[g // 2, (g % 2) * 4 + l]
    own, other = own_ref[...], other_ref[...]
    low = jnp.where(zh == 0, own, other)
    high = jnp.where(zh == 0, other, own)
    weights = jnp.concatenate([low, high], axis=1)
    for g in range(8):
        partial_ref[g] = lax.dot_general(
            rows_ref[:, g * 128 : g * 128 + 128],
            weights,
            (((0,), (1,)), ((), ())),
            preferred_element_type=F32,
        ).astype(BF)
    hid = hid_ref[...].reshape(1024, 256)
    first = lax.dot_general(hid, rows_ref[:256], (((0,), (1,)), ((), ())), preferred_element_type=F32)
    second = lax.dot_general(hid, rows_ref[256:], (((0,), (1,)), ((), ())), preferred_element_type=F32)
    keep_ref[...] = jnp.where(zh == 0, first, second)
    send_ref[...] = jnp.where(zh == 0, second, first).astype(BF)


def after(value, *deps):
    return lax.optimization_barrier((value, *deps))[0]


def gather(part, axis):
    return lax.all_to_all(jnp.broadcast_to(part[None], (lax.axis_size(axis),) + part.shape), axis, 0, 0)


def scatter_sum(parts, axis):
    return jnp.sum(lax.all_to_all(parts, axis, 0, 0).astype(F32), axis=0)


def body(gate_input, up_input, residual, down_proj, cotangent):
    swap = swap_pairs()
    cot_moved = lax.ppermute(cotangent.T, AXES, swap)
    w_other = lax.ppermute(down_proj, "zh", ACROSS)

    spread = pl.pallas_call(
        hidden_kernel,
        out_shape=shape((8, 128, 256)),
        cost_estimate=pl.CostEstimate(flops=500_000, bytes_accessed=700_000, transcendentals=0),
    )(gate_input, up_input)
    hid = lax.all_to_all(spread, "y", 0, 0)

    w_now = w_other
    keep, send = in_vmem(
        proj_kernel,
        [shape((4, 8, 64, 128))] * 2,
        2 * 1024 * 256 * 512,
        hid,
        down_proj,
        w_now,
    )
    send, cot_moved = lax.optimization_barrier((send, cot_moved))
    came = lax.ppermute(send, "c", ACROSS)
    cot_line = gather(cot_moved, "zl")

    (packed,) = in_vmem(pack_kernel, [shape((4, 16, 64, 128))], 300_000, cot_line, keep, came)
    mine, proj = in_vmem(
        unpack_kernel,
        [shape((4, 8, 64, 128)), shape((8, 64, 128))],
        300_000,
        lax.all_to_all(packed, "x", 0, 0),
    )
    its = lax.ppermute(mine, "c", ACROSS)
    proj = scatter_sum(proj, "zl")
    partial, term, term_out = in_vmem(
        grad_kernel,
        [shape((8, 128, 256)), shape((256, 256), F32), shape((256, 256))],
        4 * 1024 * 256 * 512,
        hid,
        mine,
        its,
        down_proj,
        w_now,
        scratch=[pltpu.VMEM((512, 1024), BF)],
    )
    moved = lax.ppermute(proj, AXES, swap)
    term_in = lax.ppermute(after(term_out, proj), "zh", ACROSS)
    hidden_grad = scatter_sum(after(partial, proj), "y")

    gate = gate_input.astype(F32)
    up = up_input.astype(F32)
    sig = jax.nn.sigmoid(gate)
    up_grad = (hidden_grad * gate * sig).astype(BF)
    gate_grad = (hidden_grad * up * sig * (1.0 + gate * (1.0 - sig))).astype(BF)
    down_grad = ((term + term_in.astype(F32)) * (1.0 / math.sqrt(2048))).astype(BF)
    layer_out = (after(residual, down_grad).astype(F32).T + moved).astype(BF).T
    return (layer_out, gate_grad, up_grad, down_grad)


def solution(mesh):
    fine = Mesh(mesh.devices.reshape(SIZES), AXES)
    dp, tensor = ("y", "zh"), ("x", "zl", "c")
    in_specs = (P(dp, tensor), P(dp, tensor), P(dp, tensor), P(tensor, dp), P(dp, tensor))
    out_specs = (P(dp, tensor), P(dp, tensor), P(dp, tensor), P(tensor, dp))
    return jax.shard_map(body, mesh=fine, in_specs=in_specs, out_specs=out_specs, check_vma=False)
```

```python
import math

import jax
import jax.numpy as jnp
from jax import lax
from jax.experimental import pallas as pl
from jax.experimental.pallas import tpu as pltpu
from jax.sharding import Mesh
from jax.sharding import PartitionSpec as P

AXES = ("y", "zh", "x", "zl", "c")
SIZES = (8, 2, 4, 8, 2)
BF, F32 = jnp.bfloat16, jnp.float32
ACROSS = [(0, 1), (1, 0)]


def swap_pairs():
    def at(y, zh, x, zl, c):
        return (((y * 2 + zh) * 4 + x) * 8 + zl) * 2 + c

    return [
        (at(y, zh, x, zl, c), at(2 * x + zl // 4, zh, y // 2, 4 * (y % 2) + zl % 4, c))
        for y in range(8)
        for zh in range(2)
        for x in range(4)
        for zl in range(8)
        for c in range(2)
    ]


def in_vmem(kernel, out_shapes, flops, *operands, scratch=()):
    spec = pl.BlockSpec(memory_space=pltpu.VMEM)
    moved = sum(math.prod(a.shape) * a.dtype.itemsize for a in (*operands, *out_shapes))
    return pl.pallas_call(
        kernel,
        out_shape=out_shapes,
        in_specs=[spec] * len(operands),
        out_specs=[spec] * len(out_shapes),
        scratch_shapes=list(scratch),
        compiler_params=pltpu.CompilerParams(vmem_limit_bytes=32 * 1024 * 1024),
        cost_estimate=pl.CostEstimate(flops=flops, bytes_accessed=moved, transcendentals=0),
    )(*operands)


def shape(dims, dtype=BF):
    return jax.ShapeDtypeStruct(dims, dtype)


def hidden_kernel(gate_ref, up_ref, out_ref):
    gate = gate_ref[...].astype(F32)
    hidden = (gate * jax.nn.sigmoid(gate) * up_ref[...].astype(F32)).astype(BF)
    for i in range(8):
        out_ref[i] = hidden


def proj_kernel(hid_ref, own_ref, other_ref, keep_ref, send_ref):
    zh, core = lax.axis_index("zh"), lax.axis_index("c")
    hid = hid_ref[...].reshape(1024, 256)
    for l in range(4):
        cols = slice((l % 2) * 128, (l % 2) * 128 + 128)
        w = jnp.where(zh == l // 2, own_ref[:, cols], other_ref[:, cols])
        res = lax.dot_general(w, hid, (((0,), (1,)), ((), ())), preferred_element_type=F32).astype(BF)
        first, second = res[:64], res[64:]
        keep = jnp.where(core == 0, first, second)
        send = jnp.where(core == 0, second, first)
        for g in range(8):
            toks = slice(g * 128, g * 128 + 128)
            keep_ref[g // 2, (g % 2) * 4 + l] = keep[:, toks]
            send_ref[g // 2, (g % 2) * 4 + l] = send[:, toks]


def pack_kernel(cot_ref, keep_ref, came_ref, out_ref):
    total = (keep_ref[...].astype(F32) + came_ref[...].astype(F32)).astype(BF)
    for x in range(4):
        out_ref[x, :8] = cot_ref[...]
        out_ref[x, 8:] = total[x]


def unpack_kernel(got_ref, cot_ref, sum_ref):
    cot_ref[...] = got_ref[:, :8]
    sum_ref[...] = jnp.sum(got_ref[:, 8:].astype(F32), axis=0).astype(BF)


def grad_kernel(hid_ref, mine_ref, its_ref, own_ref, other_ref, partial_ref, keep_ref, send_ref, rows_ref):
    zh, core = lax.axis_index("zh"), lax.axis_index("c")
    for l in range(4):
        here = pl.ds(pl.multiple_of((2 * l + core) * 64, 64), 64)
        there = pl.ds(pl.multiple_of((2 * l + 1 - core) * 64, 64), 64)
        for g in range(8):
            toks = slice(g * 128, g * 128 + 128)
            rows_ref[here, toks] = mine_ref[g // 2, (g % 2) * 4 + l]
            rows_ref[there, toks] = its_ref[g // 2, (g % 2) * 4 + l]
    own, other = own_ref[...], other_ref[...]
    low = jnp.where(zh == 0, own, other)
    high = jnp.where(zh == 0, other, own)
    weights = jnp.concatenate([low, high], axis=1)
    for g in range(8):
        partial_ref[g] = lax.dot_general(
            rows_ref[:, g * 128 : g * 128 + 128],
            weights,
            (((0,), (1,)), ((), ())),
            preferred_element_type=F32,
        ).astype(BF)
    hid = hid_ref[...].reshape(1024, 256)
    first = lax.dot_general(hid, rows_ref[:256], (((0,), (1,)), ((), ())), preferred_element_type=F32)
    second = lax.dot_general(hid, rows_ref[256:], (((0,), (1,)), ((), ())), preferred_element_type=F32)
    keep_ref[...] = jnp.where(zh == 0, first, second)
    send_ref[...] = jnp.where(zh == 0, second, first).astype(BF)


def after(value, *deps):
    return lax.optimization_barrier((value, *deps))[0]


def gather(part, axis):
    return lax.all_to_all(jnp.broadcast_to(part[None], (lax.axis_size(axis),) + part.shape), axis, 0, 0)


def scatter_sum(parts, axis):
    return jnp.sum(lax.all_to_all(parts, axis, 0, 0).astype(F32), axis=0)


def body(gate_input, up_input, residual, down_proj, cotangent):
    swap = swap_pairs()
    cot_moved = lax.ppermute(cotangent.T, AXES, swap)
    w_other = lax.ppermute(down_proj, "zh", ACROSS)

    spread = pl.pallas_call(
        hidden_kernel,
        out_shape=shape((8, 128, 256)),
        cost_estimate=pl.CostEstimate(flops=500_000, bytes_accessed=700_000, transcendentals=0),
    )(gate_input, up_input)
    hid = lax.all_to_all(spread, "y", 0, 0)

    w_now = w_other
    keep, send = in_vmem(
        proj_kernel,
        [shape((4, 8, 64, 128))] * 2,
        2 * 1024 * 256 * 512,
        hid,
        down_proj,
        w_now,
    )
    send, cot_moved = lax.optimization_barrier((send, cot_moved))
    came = lax.ppermute(send, "c", ACROSS)
    cot_line = gather(cot_moved, "zl")

    (packed,) = in_vmem(pack_kernel, [shape((4, 16, 64, 128))], 300_000, cot_line, keep, came)
    mine, proj = in_vmem(
        unpack_kernel,
        [shape((4, 8, 64, 128)), shape((8, 64, 128))],
        300_000,
        lax.all_to_all(packed, "x", 0, 0),
    )
    its = lax.ppermute(mine, "c", ACROSS)
    proj = scatter_sum(proj, "zl")
    partial, term, term_out = in_vmem(
        grad_kernel,
        [shape((8, 128, 256)), shape((256, 256), F32), shape((256, 256))],
        4 * 1024 * 256 * 512,
        hid,
        mine,
        its,
        down_proj,
        w_now,
        scratch=[pltpu.VMEM((512, 1024), BF)],
    )
    moved = lax.ppermute(proj, AXES, swap)
    term_in = lax.ppermute(after(term_out, proj), "zh", ACROSS)
    hidden_grad = scatter_sum(after(partial, proj), "y")

    gate = gate_input.astype(F32)
    up = up_input.astype(F32)
    sig = jax.nn.sigmoid(gate)
    up_grad = (hidden_grad * gate * sig).astype(BF)
    gate_grad = (hidden_grad * up * sig * (1.0 + gate * (1.0 - sig))).astype(BF)
    down_grad = ((term + term_in.astype(F32)) * (1.0 / math.sqrt(2048))).astype(BF)
    layer_out = (after(residual, down_grad, up_grad).astype(F32).T + moved).astype(BF).T
    return (layer_out, gate_grad, up_grad, down_grad)


def solution(mesh):
    fine = Mesh(mesh.devices.reshape(SIZES), AXES)
    dp, tensor = ("y", "zh"), ("x", "zl", "c")
    in_specs = (P(dp, tensor), P(dp, tensor), P(dp, tensor), P(tensor, dp), P(dp, tensor))
    out_specs = (P(dp, tensor), P(dp, tensor), P(dp, tensor), P(tensor, dp))
    return jax.shard_map(body, mesh=fine, in_specs=in_specs, out_specs=out_specs, check_vma=False)
```
